32 devices in a mesh: groups: 2 (over x), gz: 16 (over z, y, core).
Axes of the slice: x: 2, y: 2, z: 4, core: 2. Of those that a mesh axis runs over, the one named last changes fastest.
Arguments:
- source: float32 [6, 32, 16384], P('groups', 'gz'), parts along dimension 0, may hold values from -6 to 6
- warm_start: float32 [6, 32, 16384], P('groups', 'gz'), parts along dimension 0, may hold values from -3 to 3
- coefficient: float32 [64, 16384], P(('groups', 'gz')), parts along dimension 0, may hold values from 0.1 to 10
Outputs:
- velocity: float32 [6, 32, 16384], P('groups', 'gz'), parts along dimension 0
The draws below stay inside these ranges and needn't reach their ends.
There are 2 independent parts, one for each index of `groups`. The reference program is written for one: setup_inputs(seed, part) draws one part's arguments, and reference() takes and returns one part's arrays. A program takes and returns all parts, laid end to end along the dimension named above; each array names one. Nothing has to cross between parts.
All inputs are finite; a program needn't handle non-finite values.
Results may differ from the reference program's by a relative error of at most 0.00002.
Values sent between devices are 32-bit elements; how exact they have to be, the bound alone decides.
A program may use at most 64 MiB of HBM per device.

```python
import math
import jax
import jax.numpy as jnp

NY = 8
NX = 2048
NU1 = 2
NU2 = 2
NC = 4
NZ = 32


def steps_of(stream_key, shape, split, least, top_value):
    level = 1.0
    for axis_at, shards_of in split:
        draws = jax.random.uniform(jax.random.fold_in(jax.random.fold_in(stream_key, 6), axis_at), (shards_of,), jnp.float32, least / len(split), top_value / len(split))
        level = level * jnp.repeat(jnp.exp(draws), shape[axis_at] // shards_of).reshape((-1,) + (1,) * (len(shape) - 1 - axis_at))
    return level


def normal_values(key, extent, width, limit, shards=(), kind=jnp.bfloat16):
    entries = width * jax.random.normal(key, extent, jnp.float32)
    if shards:
        entries = entries * steps_of(key, extent, shards, -0.22, 0.18)
    return jnp.clip(entries, -limit, limit).astype(kind)


def setup_inputs(seed: int = 0, part: int = 0) -> dict:
    key_of = jax.random.split(jax.random.key(seed), 4)
    part_splits = jax.random.split(jax.random.fold_in(key_of[3], part), 4)
    return {
        "source": normal_values(part_splits[0], (3, NZ, NY * NX), 1.0, 6.0, ((1, 16),), jnp.float32),
        "warm_start": normal_values(part_splits[1], (3, NZ, NY * NX), 0.5, 3.0, ((1, 16),), jnp.float32),
        "coefficient": jnp.clip(jnp.exp(math.log(10.0) - 4.6051702 * jax.random.uniform(part_splits[2], (NZ, NY * NX), jnp.float32) ** steps_of(part_splits[2], (NZ, NY * NX), ((0, 16),), -0.2, 0.2)), 0.1, 10.0),
    }


OMEGA = 0.8


def shifted(field, offset):
    lead = field.shape[:-1]
    if offset > 0:
        return jnp.concatenate([field[..., offset:], jnp.zeros(lead + (offset,), field.dtype)], axis=-1)
    return jnp.concatenate([jnp.zeros(lead + (-offset,), field.dtype), field[..., :offset]], axis=-1)


def plane_faces(coeff_ext, lower_open, upper_open, cols_x, strength):
    center = coeff_ext[1:-1]
    cells = center.shape[-1]
    rows_y = cells // cols_x
    column = jnp.arange(cells) % cols_x
    row_index = jnp.arange(cells) // cols_x
    east = jnp.where(column < cols_x - 1, 0.5 * (center + shifted(center, 1)), 0.0)
    west = jnp.where(column > 0, 0.5 * (center + shifted(center, -1)), 0.0)
    north = jnp.where(row_index < rows_y - 1, 0.5 * (center + shifted(center, cols_x)), 0.0)
    south = jnp.where(row_index > 0, 0.5 * (center + shifted(center, -cols_x)), 0.0)
    upper = jnp.where(upper_open[:, None], 0.5 * (center + coeff_ext[2:]), 0.0)
    lower = jnp.where(lower_open[:, None], 0.5 * (center + coeff_ext[:-2]), 0.0)
    diagonal = 1.0 + strength * (east + west + north + south + upper + lower)
    return (east, west, north, south, upper, lower), diagonal


def operate(field_ext, face_set, diagonal, cols_x, strength):
    field = field_ext[:, 1:-1]
    east, west, north, south, upper, lower = face_set
    pulled = east * shifted(field, 1) + west * shifted(field, -1)
    pulled = pulled + north * shifted(field, cols_x) + south * shifted(field, -cols_x)
    pulled = pulled + upper * field_ext[:, 2:] + lower * field_ext[:, :-2]
    return diagonal * field - strength * pulled


def jacobi(field_ext, target, face_set, diagonal, cols_x, strength):
    field = field_ext[:, 1:-1]
    return field + OMEGA * (target - operate(field_ext, face_set, diagonal, cols_x, strength)) / diagonal


def restrict(field, rows_y, cols_x):
    lead = field.shape[:-2]
    planes = field.shape[-2]
    blocks = field.reshape(lead + (planes // 2, 2, rows_y // 2, 2, cols_x // 2, 2))
    total = blocks.sum(axis=(-5, -3, -1))
    return 0.125 * total.reshape(lead + (planes // 2, (rows_y // 2) * (cols_x // 2)))


def prolong(correction, rows_c, cols_c):
    comps, planes, cells = correction.shape
    grid = correction.reshape(comps, planes, 1, rows_c, 1, cols_c, 1)
    wide = jnp.broadcast_to(grid, (comps, planes, 2, rows_c, 2, cols_c, 2))
    return wide.reshape(comps, 2 * planes, 4 * cells)


def zpad(field):
    widths = [(0, 0)] * field.ndim
    widths[-2] = (1, 1)
    return jnp.pad(field, widths)


def reference(source, warm_start, coefficient):
    plane_ids = jnp.arange(NZ)
    face_set, diagonal = plane_faces(zpad(coefficient), plane_ids > 0, plane_ids < NZ - 1, NX, 1.0)
    field = warm_start
    for repeat in range(NU1):
        field = jacobi(zpad(field), source, face_set, diagonal, NX, 1.0)
    fine_residual = source - operate(zpad(field), face_set, diagonal, NX, 1.0)
    coarse_rhs = restrict(fine_residual, NY, NX)
    coarse_coef = restrict(coefficient, NY, NX)
    coarse_ids = jnp.arange(NZ // 2)
    coarse_set, coarse_diag = plane_faces(zpad(coarse_coef), coarse_ids > 0, coarse_ids < NZ // 2 - 1, NX // 2, 0.25)
    correction = jnp.zeros_like(coarse_rhs)
    for repeat in range(NC):
        correction = jacobi(zpad(correction), coarse_rhs, coarse_set, coarse_diag, NX // 2, 0.25)
    field = field + prolong(correction, NY // 2, NX // 2)
    for repeat in range(NU2):
        field = jacobi(zpad(field), source, face_set, diagonal, NX, 1.0)
    return field
```

```python
import functools

import jax
import jax.numpy as jnp
from jax import lax
from jax.experimental import pallas as pl
from jax.experimental.pallas import tpu as pltpu
from jax.sharding import PartitionSpec as P

NY = 8
NX = 2048
NC = 4
OMEGA = 0.8
KEEP = 1.0 - OMEGA
TILES = NX // 128
QUARTER = TILES // 4
COMPS = 3

ID_COEF = 0
ID_CCOEF = 1
ID_FIELD = 2
ID_FLUX = ID_FIELD + 4 * COMPS
ID_CORR = ID_FLUX + COMPS
N_IDS = ID_CORR + NC * COMPS


def iotas(shape):
    row = lax.broadcasted_iota(jnp.int32, shape, len(shape) - 2)
    lane = lax.broadcasted_iota(jnp.int32, shape, len(shape) - 1)
    return row, lane


def roll_row(v, shift):
    return pltpu.roll(v, shift % 8, axis=v.ndim - 2)


def roll_lane(v, shift):
    return pltpu.roll(v, shift % 128, axis=v.ndim - 1)


def east_of(v):
    _, lane = iotas(v.shape)
    rolled = roll_lane(v, -1)
    after = jnp.concatenate([rolled[1:], rolled[:1]], axis=0)
    return jnp.where(lane == 127, after, rolled)


def west_of(v):
    _, lane = iotas(v.shape)
    rolled = roll_lane(v, 1)
    before = jnp.concatenate([rolled[-1:], rolled[:-1]], axis=0)
    return jnp.where(lane == 0, before, rolled)


def coarse_east_of(v):
    row, lane = iotas(v.shape[1:])
    rolled = roll_lane(v, -2)
    base = rolled[0]
    up = roll_row(base, -1)
    down = roll_lane(roll_row(base, 1), -1)
    last = jnp.where(row % 2 == 0, up, down)
    after = jnp.concatenate([rolled[1:], last[None]], axis=0)
    return jnp.where((lane >= 126)[None], after, rolled)


def coarse_west_of(v):
    row, lane = iotas(v.shape[1:])
    rolled = roll_lane(v, 2)
    base = rolled[-1]
    up = roll_lane(roll_row(base, -1), 1)
    down = roll_row(base, 1)
    up = jnp.where(lane == 0, 0.0, up)
    first = jnp.where(row % 2 == 0, up, down)
    before = jnp.concatenate([first[None], rolled[:-1]], axis=0)
    return jnp.where((lane < 2)[None], before, rolled)


def block_sum(v):
    row, lane = iotas((QUARTER, 8, 128))
    even_row, even_lane = (row % 2 == 0, lane % 2 == 0)
    q = [v[i * QUARTER:(i + 1) * QUARTER] for i in range(4)]

    def rows(a, b):
        x = jnp.where(even_row, a, b)
        y = jnp.where(even_row, b, a)
        return x + jnp.where(even_row, roll_row(y, -1), roll_row(y, 1))

    a, b = rows(q[0], q[1]), rows(q[2], q[3])
    x = jnp.where(even_lane, a, b)
    y = jnp.where(even_lane, b, a)
    return x + jnp.where(even_lane, roll_lane(y, -1), roll_lane(y, 1))


def widen(v):
    row, lane = iotas(v.shape)
    even_row, even_lane = (row % 2 == 0, lane % 2 == 0)
    e = jnp.where(even_row, v, roll_row(v, 1))
    o = jnp.where(even_row, roll_row(v, -1), v)
    return jnp.concatenate(
        [
            jnp.where(even_lane, e, roll_lane(e, 1)),
            jnp.where(even_lane, o, roll_lane(o, 1)),
            jnp.where(even_lane, roll_lane(e, -1), e),
            jnp.where(even_lane, roll_lane(o, -1), o),
        ],
        axis=0,
    )


def kernel(
    src_hbm, warm_hbm, coef_hbm, out_hbm,
    src_raw, warm_raw, coef_raw, out_raw,
    src, field, halo, coef, coef_halo, face_e, face_n, face_m, face_z, gain,
    ccoef, ccoef_halo, cface_e, cface_n, cface_z, cgain,
    flux, flux_halo, rhs, corr, corr_halo,
    in_sem, out_sem, send_sem, recv_sem,
):
    me = lax.axis_index("gz")
    count = lax.axis_size("gz")
    has_lo, has_up = me > 0, me < count - 1
    has = (has_lo, has_up)
    other = (me - 1, me + 1)
    comp_rows = 2 * NY * TILES

    def comp_slice(c):
        return pl.ds(c * comp_rows, comp_rows)

    coef_in = pltpu.make_async_copy(coef_hbm, coef_raw, in_sem.at[0])
    warm_in = [
        pltpu.make_async_copy(
            warm_hbm.at[comp_slice(c)], warm_raw.at[comp_slice(c)], in_sem.at[1 + c])
        for c in range(COMPS)
    ]
    src_in = [
        pltpu.make_async_copy(
            src_hbm.at[comp_slice(c)], src_raw.at[comp_slice(c)], in_sem.at[1 + COMPS + c])
        for c in range(COMPS)
    ]
    barrier = pltpu.get_barrier_semaphore()
    for d in range(2):
        @pl.when(has[d])
        def _():
            pl.semaphore_signal(
                barrier, inc=1, device_id={"gz": other[d]},
                device_id_type=pl.DeviceIdType.MESH)
    coef_in.start()
    for c in range(COMPS):
        warm_in[c].start()
    for c in range(COMPS):
        src_in[c].start()

    def copy(key, d, source, target):
        return pltpu.make_async_remote_copy(
            src_ref=source, dst_ref=target.at[1 - d],
            send_sem=send_sem.at[key, d], recv_sem=recv_sem.at[key, 1 - d],
            device_id={"gz": other[d]}, device_id_type=pl.DeviceIdType.MESH)

    sent = []

    def send(key, sources, target):
        for d in range(2):
            @pl.when(has[d])
            def _():
                copy(key, d, sources[d], target).start()
        sent.append((key, sources, target))

    def arrive(key, sources, target):
        for d in range(2):
            @pl.when(has[1 - d])
            def _():
                copy(key, d, sources[d], target).wait_recv()

    for d in range(2):
        @pl.when(jnp.logical_not(has[d]))
        def _():
            for t in range(4):
                for c in range(COMPS):
                    halo[t, c, d] = jnp.zeros((TILES, 8, 128), jnp.float32)
            coef_halo[d] = jnp.zeros((TILES, 8, 128), jnp.float32)
            ccoef_halo[d] = jnp.zeros((QUARTER, 8, 128), jnp.float32)
            for c in range(COMPS):
                flux_halo[c, d] = jnp.zeros((QUARTER, 8, 128), jnp.float32)
            for r in range(NC):
                for c in range(COMPS):
                    corr_halo[r, c, d] = jnp.zeros((QUARTER, 8, 128), jnp.float32)

    def spread(raw, first, target):
        for p in range(2):
            for x in range(TILES):
                target[p, x] = raw[pl.ds(first + 2 * x + p, NY, stride=2 * TILES), :]

    coef_in.wait()
    spread(coef_raw, 0, coef)
    warm_in[0].wait()
    spread(warm_raw, 0, field.at[0, 0])
    pl.semaphore_wait(barrier, has_lo.astype(jnp.int32) + has_up.astype(jnp.int32))

    def field_args(t, c):
        return (ID_FIELD + COMPS * t + c,
                (field.at[t, c, 0], field.at[t, c, 1]), halo.at[t, c])

    coef_args = (ID_COEF, (coef.at[0], coef.at[1]), coef_halo)
    send(*coef_args)
    send(*field_args(0, 0))
    for c in range(1, COMPS):
        warm_in[c].wait()
        spread(warm_raw, c * comp_rows, field.at[0, c])
        send(*field_args(0, c))
    ccoef[...] = 0.125 * block_sum(coef[0] + coef[1])
    ccoef_args = (ID_CCOEF, (ccoef, ccoef), ccoef_halo)
    send(*ccoef_args)

    shape = (TILES, 8, 128)
    tile = lax.broadcasted_iota(jnp.int32, shape, 0)
    row, lane = iotas(shape)
    last_column = (tile == TILES - 1) & (lane == 127)
    for p in range(2):
        a = coef[p]
        face_e[p] = jnp.where(last_column, 0.0, 0.5 * (a + east_of(a)))
        face_n[p] = jnp.where(row == NY - 1, 0.0, 0.5 * (a + roll_row(a, -1)))
    face_m[...] = 0.5 * (coef[0] + coef[1])
    for c in range(COMPS):
        src_in[c].wait()
        spread(src_raw, c * comp_rows, src.at[c])
    arrive(*coef_args)
    for p in range(2):
        z = jnp.where(has[p], 0.5 * (coef[p] + coef_halo[p]), 0.0)
        face_z[p] = z
        e, n = face_e[p], face_n[p]
        total = e + west_of(e) + n + roll_row(n, 1) + z + face_m[...]
        gain[p] = OMEGA / (1.0 + total)

    def pulled(u, p, u_other, u_halo):
        e, n = face_e[p], face_n[p]
        out = e * east_of(u) + west_of(e * u)
        out = out + n * roll_row(u, -1) + roll_row(n * u, 1)
        out = out + face_m[...] * u_other
        if u_halo is not None:
            out = out + face_z[p] * u_halo
        return out

    def sweep(u, c, u_halo):
        return [
            KEEP * u[p] + gain[p] * (src[c, p] + pulled(u[p], p, u[1 - p], u_halo[p]))
            for p in range(2)
        ]

    def flux_args(c):
        return (ID_FLUX + c, (flux.at[c, 0], flux.at[c, 1]), flux_halo.at[c])

    def corr_args(r, c):
        return (ID_CORR + COMPS * r + c, (corr.at[r, c], corr.at[r, c]), corr_halo.at[r, c])

    for c in range(COMPS):
        arrive(*field_args(0, c))
        new = sweep([field[0, c, p] for p in range(2)], c, [halo[0, c, p] for p in range(2)])
        for p in range(2):
            field[1, c, p] = new[p]
        send(*field_args(1, c))

    cshape = (QUARTER, 8, 128)
    ctile = lax.broadcasted_iota(jnp.int32, cshape, 0)
    crow, clane = iotas(cshape)
    clast = (ctile == QUARTER - 1) & (clane == 127) & (crow % 2 == 1)
    a = ccoef[...]
    e = jnp.where(clast, 0.0, 0.125 * (a + coarse_east_of(a)))
    n = jnp.where(crow >= NY - 2, 0.0, 0.125 * (a + roll_row(a, -2)))
    cface_e[...] = e
    cface_n[...] = n
    total = e + coarse_west_of(e) + n + roll_row(n, 2)
    arrive(*ccoef_args)
    for d in range(2):
        z = jnp.where(has[d], 0.125 * (a + ccoef_halo[d]), 0.0)
        cface_z[d] = z
        total = total + z
    cgain[...] = OMEGA / (1.0 + total)

    for c in range(COMPS):
        arrive(*field_args(1, c))
        new = sweep([field[1, c, p] for p in range(2)], c, [halo[1, c, p] for p in range(2)])
        for p in range(2):
            field[2, c, p] = new[p]
            flux[c, p] = block_sum(face_z[p] * new[p])
        send(*flux_args(c))

    for c in range(COMPS):
        u = [field[2, c, p] for p in range(2)]
        res = [
            src[c, p] + pulled(u[p], p, u[1 - p], None) - (OMEGA / gain[p]) * u[p]
            for p in range(2)
        ]
        rhs[c] = block_sum(res[0] + res[1])

    for c in range(COMPS):
        arrive(*flux_args(c))
        r = 0.125 * (rhs[c] + flux_halo[c, 0] + flux_halo[c, 1])
        rhs[c] = r
        corr[0, c] = cgain[...] * r
        send(*corr_args(0, c))

    for r in range(1, NC):
        send(*field_args(2, r - 1))
        for c in range(COMPS):
            u = corr[r - 1, c]
            e, n = cface_e[...], cface_n[...]
            out = e * coarse_east_of(u) + coarse_west_of(e * u)
            out = out + n * roll_row(u, -2) + roll_row(n * u, 2)
            arrive(*corr_args(r - 1, c))
            out = out + cface_z[0] * corr_halo[r - 1, c, 0] + cface_z[1] * corr_halo[r - 1, c, 1]
            corr[r, c] = KEEP * u + cgain[...] * (rhs[c] + out)
            send(*corr_args(r, c))

    for c in range(COMPS):
        add = widen(corr[NC - 1, c])
        u = [field[2, c, p] + add for p in range(2)]
        arrive(*field_args(2, c))
        arrive(*corr_args(NC - 1, c))
        u_halo = [halo[2, c, d] + widen(corr_halo[NC - 1, c, d]) for d in range(2)]
        new = sweep(u, c, u_halo)
        for p in range(2):
            field[3, c, p] = new[p]
        send(*field_args(3, c))

    outs = []
    for c in range(COMPS):
        arrive(*field_args(3, c))
        new = sweep([field[3, c, p] for p in range(2)], c, [halo[3, c, p] for p in range(2)])
        for p in range(2):
            for x in range(TILES):
                out_raw[pl.ds(c * comp_rows + 2 * x + p, NY, stride=2 * TILES), :] = new[p][x]
        done = pltpu.make_async_copy(
            out_raw.at[comp_slice(c)], out_hbm.at[comp_slice(c)], out_sem.at[c])
        done.start()
        outs.append(done)
    for key, sources, target in sent:
        for d in range(2):
            @pl.when(has[d])
            def _():
                copy(key, d, sources[d], target).wait_send()
    for done in outs:
        done.wait()


def body(source, warm_start, coefficient):
    comps, planes, cells = source.shape
    rows = planes * cells // 128

    def flat(array):
        lead = array.shape[:-2]
        split = array.reshape(lead + (planes, cells // 128, 128))
        return jnp.swapaxes(split, -3, -2).reshape(-1, 128)

    def vm(*shape):
        return pltpu.VMEM(shape + (8, 128), jnp.float32)

    raw = pltpu.VMEM((comps * rows, 128), jnp.float32)
    out = pl.pallas_call(
        kernel,
        out_shape=jax.ShapeDtypeStruct((comps * rows, 128), jnp.float32),
        in_specs=[pl.BlockSpec(memory_space=pl.ANY)] * 3,
        out_specs=pl.BlockSpec(memory_space=pl.ANY),
        scratch_shapes=[
            raw, raw, pltpu.VMEM((rows, 128), jnp.float32), raw,
            vm(comps, 2, TILES),
            vm(4, comps, 2, TILES),
            vm(4, comps, 2, TILES),
            vm(2, TILES), vm(2, TILES),
            vm(2, TILES), vm(2, TILES), vm(TILES), vm(2, TILES), vm(2, TILES),
            vm(QUARTER), vm(2, QUARTER),
            vm(QUARTER), vm(QUARTER), vm(2, QUARTER), vm(QUARTER),
            vm(comps, 2, QUARTER), vm(comps, 2, QUARTER),
            vm(comps, QUARTER),
            vm(NC, comps, QUARTER), vm(NC, comps, 2, QUARTER),
            pltpu.SemaphoreType.DMA((1 + 2 * COMPS,)),
            pltpu.SemaphoreType.DMA((COMPS,)),
            pltpu.SemaphoreType.DMA((N_IDS, 2)),
            pltpu.SemaphoreType.DMA((N_IDS, 2)),
        ],
        compiler_params=pltpu.CompilerParams(
            collective_id=0, has_side_effects=True, vmem_limit_bytes=48 * 1024 * 1024),
    )(flat(source), flat(warm_start), flat(coefficient))
    out = out.reshape(comps, cells // 128, planes, 128)
    return jnp.swapaxes(out, 1, 2).reshape(comps, planes, cells)


def solution(mesh):
    in_specs = (P("groups", "gz", None), P("groups", "gz", None), P(("groups", "gz"), None))
    out_specs = P("groups", "gz", None)
    return jax.shard_map(body, mesh=mesh, in_specs=in_specs, out_specs=out_specs, check_vma=False)
```

```python
import functools

import jax
import jax.numpy as jnp
from jax import lax
from jax.experimental import pallas as pl
from jax.experimental.pallas import tpu as pltpu
from jax.sharding import PartitionSpec as P

NY = 8
NX = 2048
NC = 4
OMEGA = 0.8
KEEP = 1.0 - OMEGA
TILES = NX // 128
QUARTER = TILES // 4
COMPS = 3
PIECES = 2
PIECE = TILES // PIECES
SLOTS = (2, 1, 1, 1, 1)

ID_COEF = 0
ID_CCOEF = 1
ID_FIELD = 2
ID_FLUX = ID_FIELD + 4 * COMPS * PIECES
ID_CORR = ID_FLUX + COMPS
N_IDS = ID_CORR + NC * COMPS


def iotas(shape):
    row = lax.broadcasted_iota(jnp.int32, shape, len(shape) - 2)
    lane = lax.broadcasted_iota(jnp.int32, shape, len(shape) - 1)
    return row, lane


def roll_row(v, shift):
    return pltpu.roll(v, shift % 8, axis=v.ndim - 2)


def roll_lane(v, shift):
    return pltpu.roll(v, shift % 128, axis=v.ndim - 1)


def east_of(v):
    _, lane = iotas(v.shape)
    rolled = roll_lane(v, -1)
    after = jnp.concatenate([rolled[1:], rolled[:1]], axis=0)
    return jnp.where(lane == 127, after, rolled)


def west_of(v):
    _, lane = iotas(v.shape)
    rolled = roll_lane(v, 1)
    before = jnp.concatenate([rolled[-1:], rolled[:-1]], axis=0)
    return jnp.where(lane == 0, before, rolled)


def coarse_east_of(v):
    row, lane = iotas(v.shape[1:])
    rolled = roll_lane(v, -2)
    base = rolled[0]
    up = roll_row(base, -1)
    down = roll_lane(roll_row(base, 1), -1)
    last = jnp.where(row % 2 == 0, up, down)
    after = jnp.concatenate([rolled[1:], last[None]], axis=0)
    return jnp.where((lane >= 126)[None], after, rolled)


def coarse_west_of(v):
    row, lane = iotas(v.shape[1:])
    rolled = roll_lane(v, 2)
    base = rolled[-1]
    up = roll_lane(roll_row(base, -1), 1)
    down = roll_row(base, 1)
    up = jnp.where(lane == 0, 0.0, up)
    first = jnp.where(row % 2 == 0, up, down)
    before = jnp.concatenate([first[None], rolled[:-1]], axis=0)
    return jnp.where((lane < 2)[None], before, rolled)


def block_sum(v):
    row, lane = iotas((QUARTER, 8, 128))
    even_row, even_lane = (row % 2 == 0, lane % 2 == 0)
    q = [v[i * QUARTER:(i + 1) * QUARTER] for i in range(4)]

    def rows(a, b):
        x = jnp.where(even_row, a, b)
        y = jnp.where(even_row, b, a)
        return x + jnp.where(even_row, roll_row(y, -1), roll_row(y, 1))

    a, b = rows(q[0], q[1]), rows(q[2], q[3])
    x = jnp.where(even_lane, a, b)
    y = jnp.where(even_lane, b, a)
    return x + jnp.where(even_lane, roll_lane(y, -1), roll_lane(y, 1))


def widen(v):
    row, lane = iotas(v.shape)
    even_row, even_lane = (row % 2 == 0, lane % 2 == 0)
    e = jnp.where(even_row, v, roll_row(v, 1))
    o = jnp.where(even_row, roll_row(v, -1), v)
    return jnp.concatenate(
        [
            jnp.where(even_lane, e, roll_lane(e, 1)),
            jnp.where(even_lane, o, roll_lane(o, 1)),
            jnp.where(even_lane, roll_lane(e, -1), e),
            jnp.where(even_lane, roll_lane(o, -1), o),
        ],
        axis=0,
    )


def kernel(
    src_hbm, warm_hbm, coef_hbm, out_hbm,
    src_raw, warm_raw, coef_raw, out_raw,
    src, field, halo, coef, coef_halo, face_e, face_n, face_m, face_z, gain,
    ccoef, ccoef_halo, cface_e, cface_n, cface_z, cgain,
    flux, flux_halo, rhs, corr, corr_halo,
    in_sem, out_sem, send_sem, recv_sem,
):
    me = lax.axis_index("gz")
    count = lax.axis_size("gz")
    has_lo, has_up = me > 0, me < count - 1
    has = (has_lo, has_up)
    other = (me - 1, me + 1)
    comp_rows = 2 * NY * TILES

    def comp_slice(c):
        return pl.ds(c * comp_rows, comp_rows)

    coef_in = pltpu.make_async_copy(coef_hbm, coef_raw, in_sem.at[0])
    warm_in = [
        pltpu.make_async_copy(
            warm_hbm.at[comp_slice(c)], warm_raw.at[comp_slice(c)], in_sem.at[1 + c])
        for c in range(COMPS)
    ]
    src_in = [
        pltpu.make_async_copy(
            src_hbm.at[comp_slice(c)], src_raw.at[comp_slice(c)], in_sem.at[1 + COMPS + c])
        for c in range(COMPS)
    ]
    barrier = pltpu.get_barrier_semaphore()
    for d in range(2):
        @pl.when(has[d])
        def _():
            pl.semaphore_signal(
                barrier, inc=1, device_id={"gz": other[d]},
                device_id_type=pl.DeviceIdType.MESH)
    coef_in.start()
    for c in range(COMPS):
        warm_in[c].start()
    for c in range(COMPS):
        src_in[c].start()

    def copy(key, d, source, target):
        return pltpu.make_async_remote_copy(
            src_ref=source, dst_ref=target.at[1 - d],
            send_sem=send_sem.at[key, d], recv_sem=recv_sem.at[key, 1 - d],
            device_id={"gz": other[d]}, device_id_type=pl.DeviceIdType.MESH)

    sent = []

    def send(key, sources, target):
        for d in range(2):
            @pl.when(has[d])
            def _():
                copy(key, d, sources[d], target).start()
        sent.append((key, sources, target))

    def arrive(key, sources, target):
        for d in range(2):
            @pl.when(has[1 - d])
            def _():
                copy(key, d, sources[d], target).wait_recv()

    for d in range(2):
        @pl.when(jnp.logical_not(has[d]))
        def _():
            for t in range(4):
                for c in range(COMPS):
                    halo[t, d, c] = jnp.zeros((TILES, 8, 128), jnp.float32)
            coef_halo[d] = jnp.zeros((TILES, 8, 128), jnp.float32)
            ccoef_halo[d] = jnp.zeros((QUARTER, 8, 128), jnp.float32)
            for c in range(COMPS):
                flux_halo[c, d] = jnp.zeros((QUARTER, 8, 128), jnp.float32)
            for r in range(NC):
                for c in range(COMPS):
                    corr_halo[r, d, c] = jnp.zeros((QUARTER, 8, 128), jnp.float32)

    def spread(raw, first, target):
        for p in range(2):
            for x in range(TILES):
                target[p, x] = raw[pl.ds(first + 2 * x + p, NY, stride=2 * TILES), :]

    coef_in.wait()
    spread(coef_raw, 0, coef)
    warm_in[0].wait()
    spread(warm_raw, 0, field.at[0, 0])
    pl.semaphore_wait(barrier, has_lo.astype(jnp.int32) + has_up.astype(jnp.int32))

    def field_args(t, c, h):
        tiles = pl.ds(h * PIECE, PIECE)
        return (ID_FIELD + (COMPS * t + c) * PIECES + h,
                (field.at[t, c, 0, tiles], field.at[t, c, 1, tiles]), halo.at[t, :, c, tiles])

    def send_field(t, c):
        for h in range(PIECES):
            send(*field_args(t, c, h))

    smoothed = [(c, h) for c in range(COMPS) for h in range(PIECES)]

    def send_smoothed(slot):
        first = sum(SLOTS[:slot])
        for c, h in smoothed[first:first + SLOTS[slot]]:
            send(*field_args(2, c, h))

    coef_args = (ID_COEF, (coef.at[0], coef.at[1]), coef_halo)
    send(*coef_args)
    send_field(0, 0)
    for c in range(1, COMPS):
        warm_in[c].wait()
        spread(warm_raw, c * comp_rows, field.at[0, c])
        send_field(0, c)
    ccoef[...] = 0.125 * block_sum(coef[0] + coef[1])
    ccoef_args = (ID_CCOEF, (ccoef, ccoef), ccoef_halo)

    shape = (TILES, 8, 128)
    tile = lax.broadcasted_iota(jnp.int32, shape, 0)
    row, lane = iotas(shape)
    last_column = (tile == TILES - 1) & (lane == 127)
    for p in range(2):
        a = coef[p]
        face_e[p] = jnp.where(last_column, 0.0, 0.5 * (a + east_of(a)))
        face_n[p] = jnp.where(row == NY - 1, 0.0, 0.5 * (a + roll_row(a, -1)))
    face_m[...] = 0.5 * (coef[0] + coef[1])
    for c in range(COMPS):
        src_in[c].wait()
        spread(src_raw, c * comp_rows, src.at[c])
    arrive(*coef_args)
    for p in range(2):
        z = jnp.where(has[p], 0.5 * (coef[p] + coef_halo[p]), 0.0)
        face_z[p] = z
        e, n = face_e[p], face_n[p]
        total = e + west_of(e) + n + roll_row(n, 1) + z + face_m[...]
        gain[p] = OMEGA / (1.0 + total)

    def pulled(u, p):
        e, n = face_e[p], face_n[p]
        out = e * east_of(u[p]) + west_of(e * u[p])
        out = out + n * roll_row(u[p], -1) + roll_row(n * u[p], 1)
        return out + face_m[...] * u[1 - p]

    def sweep_own(u, c):
        return [KEEP * u[p] + gain[p] * (src[c, p] + pulled(u, p)) for p in range(2)]

    def sweep_rest(own, t, c, h, wide):
        tiles = slice(h * PIECE, (h + 1) * PIECE)
        new = []
        for p in range(2):
            u_halo = halo[t, p, c, tiles]
            if wide is not None:
                u_halo = u_halo + wide[p][tiles]
            new.append(own[p][tiles] + gain[p, tiles] * (face_z[p, tiles] * u_halo))
        return new

    def next_field(t, c, own, wide=None):
        for h in range(PIECES):
            arrive(*field_args(t, c, h))
            new = sweep_rest(own, t, c, h, wide)
            for p in range(2):
                field[t + 1, c, p, h * PIECE:(h + 1) * PIECE] = new[p]
            if t != 1:
                send(*field_args(t + 1, c, h))

    def flux_args(c):
        return (ID_FLUX + c, (flux.at[c, 0], flux.at[c, 1]), flux_halo.at[c])

    def corr_args(r, c):
        return (ID_CORR + COMPS * r + c, (corr.at[r, c], corr.at[r, c]), corr_halo.at[r, :, c])

    for c in range(COMPS):
        next_field(0, c, sweep_own([field[0, c, p] for p in range(2)], c))
    send(*ccoef_args)

    for c in range(COMPS):
        next_field(1, c, sweep_own([field[1, c, p] for p in range(2)], c))
        for p in range(2):
            flux[c, p] = block_sum(face_z[p] * field[2, c, p])
        send(*flux_args(c))

    send_smoothed(0)
    for c in range(COMPS):
        u = [field[2, c, p] for p in range(2)]
        res = [
            src[c, p] + pulled(u, p) - (OMEGA / gain[p]) * u[p]
            for p in range(2)
        ]
        rhs[c] = block_sum(res[0] + res[1])

    cshape = (QUARTER, 8, 128)
    ctile = lax.broadcasted_iota(jnp.int32, cshape, 0)
    crow, clane = iotas(cshape)
    clast = (ctile == QUARTER - 1) & (clane == 127) & (crow % 2 == 1)
    a = ccoef[...]
    e = jnp.where(clast, 0.0, 0.125 * (a + coarse_east_of(a)))
    n = jnp.where(crow >= NY - 2, 0.0, 0.125 * (a + roll_row(a, -2)))
    cface_e[...] = e
    cface_n[...] = n
    total = e + coarse_west_of(e) + n + roll_row(n, 2)
    arrive(*ccoef_args)
    for d in range(2):
        z = jnp.where(has[d], 0.125 * (a + ccoef_halo[d]), 0.0)
        cface_z[d] = z
        total = total + z
    cgain[...] = OMEGA / (1.0 + total)

    for c in range(COMPS):
        arrive(*flux_args(c))
        r = 0.125 * (rhs[c] + flux_halo[c, 0] + flux_halo[c, 1])
        rhs[c] = r
        corr[0, c] = cgain[...] * r
        send(*corr_args(0, c))

    for r in range(1, NC):
        send_smoothed(r)
        own = []
        for c in range(COMPS):
            u = corr[r - 1, c]
            e, n = cface_e[...], cface_n[...]
            out = e * coarse_east_of(u) + coarse_west_of(e * u)
            out = out + n * roll_row(u, -2) + roll_row(n * u, 2)
            own.append(KEEP * u + cgain[...] * (rhs[c] + out))
        for c in range(COMPS):
            arrive(*corr_args(r - 1, c))
            out = cface_z[0] * corr_halo[r - 1, 0, c] + cface_z[1] * corr_halo[r - 1, 1, c]
            corr[r, c] = own[c] + cgain[...] * out
            send(*corr_args(r, c))

    send_smoothed(NC)
    for c in range(COMPS):
        add = widen(corr[NC - 1, c])
        own = sweep_own([field[2, c, p] + add for p in range(2)], c)
        arrive(*corr_args(NC - 1, c))
        next_field(2, c, own, [widen(corr_halo[NC - 1, d, c]) for d in range(2)])

    outs = []
    for c in range(COMPS):
        own = sweep_own([field[3, c, p] for p in range(2)], c)
        for h in range(PIECES):
            arrive(*field_args(3, c, h))
            new = sweep_rest(own, 3, c, h, None)
            for p in range(2):
                for x in range(PIECE):
                    first = c * comp_rows + 2 * (h * PIECE + x) + p
                    out_raw[pl.ds(first, NY, stride=2 * TILES), :] = new[p][x]
        done = pltpu.make_async_copy(
            out_raw.at[comp_slice(c)], out_hbm.at[comp_slice(c)], out_sem.at[c])
        done.start()
        outs.append(done)
    for key, sources, target in sent:
        for d in range(2):
            @pl.when(has[d])
            def _():
                copy(key, d, sources[d], target).wait_send()
    for done in outs:
        done.wait()


def body(source, warm_start, coefficient):
    comps, planes, cells = source.shape
    rows = planes * cells // 128

    def flat(array):
        lead = array.shape[:-2]
        split = array.reshape(lead + (planes, cells // 128, 128))
        return jnp.swapaxes(split, -3, -2).reshape(-1, 128)

    def vm(*shape):
        return pltpu.VMEM(shape + (8, 128), jnp.float32)

    raw = pltpu.VMEM((comps * rows, 128), jnp.float32)
    out = pl.pallas_call(
        kernel,
        out_shape=jax.ShapeDtypeStruct((comps * rows, 128), jnp.float32),
        in_specs=[pl.BlockSpec(memory_space=pl.ANY)] * 3,
        out_specs=pl.BlockSpec(memory_space=pl.ANY),
        scratch_shapes=[
            raw, raw, pltpu.VMEM((rows, 128), jnp.float32), raw,
            vm(comps, 2, TILES),
            vm(4, comps, 2, TILES),
            vm(4, 2, comps, TILES),
            vm(2, TILES), vm(2, TILES),
            vm(2, TILES), vm(2, TILES), vm(TILES), vm(2, TILES), vm(2, TILES),
            vm(QUARTER), vm(2, QUARTER),
            vm(QUARTER), vm(QUARTER), vm(2, QUARTER), vm(QUARTER),
            vm(comps, 2, QUARTER), vm(comps, 2, QUARTER),
            vm(comps, QUARTER),
            vm(NC, comps, QUARTER), vm(NC, 2, comps, QUARTER),
            pltpu.SemaphoreType.DMA((1 + 2 * COMPS,)),
            pltpu.SemaphoreType.DMA((COMPS,)),
            pltpu.SemaphoreType.DMA((N_IDS, 2)),
            pltpu.SemaphoreType.DMA((N_IDS, 2)),
        ],
        compiler_params=pltpu.CompilerParams(
            collective_id=0, has_side_effects=True, vmem_limit_bytes=54528 * 1024),
    )(flat(source), flat(warm_start), flat(coefficient))
    out = out.reshape(comps, cells // 128, planes, 128)
    return jnp.swapaxes(out, 1, 2).reshape(comps, planes, cells)


def solution(mesh):
    in_specs = (P("groups", "gz", None), P("groups", "gz", None), P(("groups", "gz"), None))
    out_specs = P("groups", "gz", None)
    return jax.shard_map(body, mesh=mesh, in_specs=in_specs, out_specs=out_specs, check_vma=False)
```

```python
import functools

import jax
import jax.numpy as jnp
from jax import lax
from jax.experimental import pallas as pl
from jax.experimental.pallas import tpu as pltpu
from jax.sharding import PartitionSpec as P

NY = 8
NX = 2048
NC = 4
OMEGA = 0.8
KEEP = 1.0 - OMEGA
TILES = NX // 128
QUARTER = TILES // 4
COMPS = 3
PIECES = 2
PIECE = TILES // PIECES
SLOTS = (2, 1, 1, 1, 1)

ID_COEF = 0
ID_CCOEF = 1
ID_FIELD = 2
ID_FLUX = ID_FIELD + 4 * COMPS * PIECES
ID_CORR = ID_FLUX + COMPS
N_IDS = ID_CORR + NC * COMPS


def iotas(shape):
    row = lax.broadcasted_iota(jnp.int32, shape, len(shape) - 2)
    lane = lax.broadcasted_iota(jnp.int32, shape, len(shape) - 1)
    return row, lane


def roll_row(v, shift):
    return pltpu.roll(v, shift % 8, axis=v.ndim - 2)


def roll_lane(v, shift):
    return pltpu.roll(v, shift % 128, axis=v.ndim - 1)


def east_of(v):
    _, lane = iotas(v.shape)
    rolled = roll_lane(v, -1)
    after = jnp.concatenate([rolled[1:], rolled[:1]], axis=0)
    return jnp.where(lane == 127, after, rolled)


def west_of(v):
    _, lane = iotas(v.shape)
    rolled = roll_lane(v, 1)
    before = jnp.concatenate([rolled[-1:], rolled[:-1]], axis=0)
    return jnp.where(lane == 0, before, rolled)


def coarse_east_of(v):
    row, lane = iotas(v.shape[1:])
    rolled = roll_lane(v, -2)
    base = rolled[0]
    up = roll_row(base, -1)
    down = roll_lane(roll_row(base, 1), -1)
    last = jnp.where(row % 2 == 0, up, down)
    after = jnp.concatenate([rolled[1:], last[None]], axis=0)
    return jnp.where((lane >= 126)[None], after, rolled)


def coarse_west_of(v):
    row, lane = iotas(v.shape[1:])
    rolled = roll_lane(v, 2)
    base = rolled[-1]
    up = roll_lane(roll_row(base, -1), 1)
    down = roll_row(base, 1)
    up = jnp.where(lane == 0, 0.0, up)
    first = jnp.where(row % 2 == 0, up, down)
    before = jnp.concatenate([first[None], rolled[:-1]], axis=0)
    return jnp.where((lane < 2)[None], before, rolled)


def block_sum(v):
    row, lane = iotas((QUARTER, 8, 128))
    even_row, even_lane = (row % 2 == 0, lane % 2 == 0)
    q = [v[i * QUARTER:(i + 1) * QUARTER] for i in range(4)]

    def rows(a, b):
        x = jnp.where(even_row, a, b)
        y = jnp.where(even_row, b, a)
        return x + jnp.where(even_row, roll_row(y, -1), roll_row(y, 1))

    a, b = rows(q[0], q[1]), rows(q[2], q[3])
    x = jnp.where(even_lane, a, b)
    y = jnp.where(even_lane, b, a)
    return x + jnp.where(even_lane, roll_lane(y, -1), roll_lane(y, 1))


def widen(v):
    row, lane = iotas(v.shape)
    even_row, even_lane = (row % 2 == 0, lane % 2 == 0)
    e = jnp.where(even_row, v, roll_row(v, 1))
    o = jnp.where(even_row, roll_row(v, -1), v)
    return jnp.concatenate(
        [
            jnp.where(even_lane, e, roll_lane(e, 1)),
            jnp.where(even_lane, o, roll_lane(o, 1)),
            jnp.where(even_lane, roll_lane(e, -1), e),
            jnp.where(even_lane, roll_lane(o, -1), o),
        ],
        axis=0,
    )


def kernel(
    src_hbm, warm_hbm, coef_hbm, out_hbm,
    src_raw, warm_raw, coef_raw, out_raw,
    src, field, halo, coef, coef_halo, face_e, face_n, face_m, face_z, gain,
    ccoef, ccoef_halo, cface_e, cface_n, cface_z, cgain,
    flux, flux_halo, rhs, corr, corr_halo,
    in_sem, out_sem, send_sem, recv_sem,
):
    me = lax.axis_index("gz")
    count = lax.axis_size("gz")
    has_lo, has_up = me > 0, me < count - 1
    has = (has_lo, has_up)
    other = (me - 1, me + 1)
    comp_rows = 2 * NY * TILES

    def comp_slice(c):
        return pl.ds(c * comp_rows, comp_rows)

    coef_in = pltpu.make_async_copy(coef_hbm, coef_raw, in_sem.at[0])
    warm_in = [
        pltpu.make_async_copy(
            warm_hbm.at[comp_slice(c)], warm_raw.at[comp_slice(c)], in_sem.at[1 + c])
        for c in range(COMPS)
    ]
    src_in = [
        pltpu.make_async_copy(
            src_hbm.at[comp_slice(c)], src_raw.at[comp_slice(c)], in_sem.at[1 + COMPS + c])
        for c in range(COMPS)
    ]
    barrier = pltpu.get_barrier_semaphore()
    for d in range(2):
        @pl.when(has[d])
        def _():
            pl.semaphore_signal(
                barrier, inc=1, device_id={"gz": other[d]},
                device_id_type=pl.DeviceIdType.MESH)
    coef_in.start()
    for c in range(COMPS):
        warm_in[c].start()
    for c in range(COMPS):
        src_in[c].start()

    def copy(key, d, source, target):
        return pltpu.make_async_remote_copy(
            src_ref=source, dst_ref=target.at[1 - d],
            send_sem=send_sem.at[key, d], recv_sem=recv_sem.at[key, 1 - d],
            device_id={"gz": other[d]}, device_id_type=pl.DeviceIdType.MESH)

    sent = []

    def send(key, sources, target):
        for d in range(2):
            @pl.when(has[d])
            def _():
                copy(key, d, sources[d], target).start()
        sent.append((key, sources, target))

    def arrive(key, sources, target):
        for d in range(2):
            @pl.when(has[1 - d])
            def _():
                copy(key, d, sources[d], target).wait_recv()

    def drain(keep=0):
        while len(sent) > keep:
            key, sources, target = sent.pop(0)
            for d in range(2):
                @pl.when(has[d])
                def _():
                    copy(key, d, sources[d], target).wait_send()

    for d in range(2):
        @pl.when(jnp.logical_not(has[d]))
        def _():
            for t in range(4):
                for c in range(COMPS):
                    halo[t, d, c] = jnp.zeros((TILES, 8, 128), jnp.float32)
            coef_halo[d] = jnp.zeros((TILES, 8, 128), jnp.float32)
            ccoef_halo[d] = jnp.zeros((QUARTER, 8, 128), jnp.float32)
            for c in range(COMPS):
                flux_halo[c, d] = jnp.zeros((QUARTER, 8, 128), jnp.float32)
            for r in range(NC):
                for c in range(COMPS):
                    corr_halo[r, d, c] = jnp.zeros((QUARTER, 8, 128), jnp.float32)

    def spread(raw, first, target):
        for p in range(2):
            for x in range(TILES):
                target[p, x] = raw[pl.ds(first + 2 * x + p, NY, stride=2 * TILES), :]

    coef_in.wait()
    spread(coef_raw, 0, coef)
    warm_in[0].wait()
    spread(warm_raw, 0, field.at[0, 0])
    pl.semaphore_wait(barrier, has_lo.astype(jnp.int32) + has_up.astype(jnp.int32))

    def field_args(t, c, h):
        tiles = pl.ds(h * PIECE, PIECE)
        return (ID_FIELD + (COMPS * t + c) * PIECES + h,
                (field.at[t, c, 0, tiles], field.at[t, c, 1, tiles]), halo.at[t, :, c, tiles])

    def send_field(t, c):
        for h in range(PIECES):
            send(*field_args(t, c, h))

    smoothed = [(c, h) for c in range(COMPS) for h in range(PIECES)]

    def send_smoothed(slot):
        first = sum(SLOTS[:slot])
        for c, h in smoothed[first:first + SLOTS[slot]]:
            send(*field_args(2, c, h))

    coef_args = (ID_COEF, (coef.at[0], coef.at[1]), coef_halo)
    send(*coef_args)
    send_field(0, 0)
    for c in range(1, COMPS):
        warm_in[c].wait()
        spread(warm_raw, c * comp_rows, field.at[0, c])
        send_field(0, c)
    ccoef[...] = 0.125 * block_sum(coef[0] + coef[1])
    ccoef_args = (ID_CCOEF, (ccoef, ccoef), ccoef_halo)

    shape = (TILES, 8, 128)
    tile = lax.broadcasted_iota(jnp.int32, shape, 0)
    row, lane = iotas(shape)
    last_column = (tile == TILES - 1) & (lane == 127)
    for p in range(2):
        a = coef[p]
        face_e[p] = jnp.where(last_column, 0.0, 0.5 * (a + east_of(a)))
        face_n[p] = jnp.where(row == NY - 1, 0.0, 0.5 * (a + roll_row(a, -1)))
    face_m[...] = 0.5 * (coef[0] + coef[1])
    for c in range(COMPS):
        src_in[c].wait()
        spread(src_raw, c * comp_rows, src.at[c])
    arrive(*coef_args)
    for p in range(2):
        z = jnp.where(has[p], 0.5 * (coef[p] + coef_halo[p]), 0.0)
        face_z[p] = z
        e, n = face_e[p], face_n[p]
        total = e + west_of(e) + n + roll_row(n, 1) + z + face_m[...]
        gain[p] = OMEGA / (1.0 + total)

    def pulled(u, p):
        e, n = face_e[p], face_n[p]
        out = e * east_of(u[p]) + west_of(e * u[p])
        out = out + n * roll_row(u[p], -1) + roll_row(n * u[p], 1)
        return out + face_m[...] * u[1 - p]

    def sweep_own(u, c):
        return [KEEP * u[p] + gain[p] * (src[c, p] + pulled(u, p)) for p in range(2)]

    def sweep_rest(own, t, c, h, wide):
        tiles = slice(h * PIECE, (h + 1) * PIECE)
        new = []
        for p in range(2):
            u_halo = halo[t, p, c, tiles]
            if wide is not None:
                u_halo = u_halo + wide[p][tiles]
            new.append(own[p][tiles] + gain[p, tiles] * (face_z[p, tiles] * u_halo))
        return new

    def next_field(t, c, own, wide=None):
        for h in range(PIECES):
            arrive(*field_args(t, c, h))
            new = sweep_rest(own, t, c, h, wide)
            for p in range(2):
                field[t + 1, c, p, h * PIECE:(h + 1) * PIECE] = new[p]
            if t != 1:
                send(*field_args(t + 1, c, h))

    def flux_args(c):
        return (ID_FLUX + c, (flux.at[c, 0], flux.at[c, 1]), flux_halo.at[c])

    def corr_args(r, c):
        return (ID_CORR + COMPS * r + c, (corr.at[r, c], corr.at[r, c]), corr_halo.at[r, :, c])

    for c in range(COMPS):
        next_field(0, c, sweep_own([field[0, c, p] for p in range(2)], c))
    send(*ccoef_args)

    for c in range(COMPS):
        next_field(1, c, sweep_own([field[1, c, p] for p in range(2)], c))
        for p in range(2):
            flux[c, p] = block_sum(face_z[p] * field[2, c, p])
        send(*flux_args(c))

    send_smoothed(0)
    for c in range(COMPS):
        u = [field[2, c, p] for p in range(2)]
        res = [
            src[c, p] + pulled(u, p) - (OMEGA / gain[p]) * u[p]
            for p in range(2)
        ]
        rhs[c] = block_sum(res[0] + res[1])

    cshape = (QUARTER, 8, 128)
    ctile = lax.broadcasted_iota(jnp.int32, cshape, 0)
    crow, clane = iotas(cshape)
    clast = (ctile == QUARTER - 1) & (clane == 127) & (crow % 2 == 1)
    a = ccoef[...]
    e = jnp.where(clast, 0.0, 0.125 * (a + coarse_east_of(a)))
    n = jnp.where(crow >= NY - 2, 0.0, 0.125 * (a + roll_row(a, -2)))
    cface_e[...] = e
    cface_n[...] = n
    total = e + coarse_west_of(e) + n + roll_row(n, 2)
    arrive(*ccoef_args)
    for d in range(2):
        z = jnp.where(has[d], 0.125 * (a + ccoef_halo[d]), 0.0)
        cface_z[d] = z
        total = total + z
    cgain[...] = OMEGA / (1.0 + total)

    for c in range(COMPS):
        arrive(*flux_args(c))
        r = 0.125 * (rhs[c] + flux_halo[c, 0] + flux_halo[c, 1])
        rhs[c] = r
        corr[0, c] = cgain[...] * r
        send(*corr_args(0, c))

    for r in range(1, NC):
        send_smoothed(r)
        own = []
        for c in range(COMPS):
            u = corr[r - 1, c]
            e, n = cface_e[...], cface_n[...]
            out = e * coarse_east_of(u) + coarse_west_of(e * u)
            out = out + n * roll_row(u, -2) + roll_row(n * u, 2)
            own.append(KEEP * u + cgain[...] * (rhs[c] + out))
        for c in range(COMPS):
            arrive(*corr_args(r - 1, c))
            out = cface_z[0] * corr_halo[r - 1, 0, c] + cface_z[1] * corr_halo[r - 1, 1, c]
            corr[r, c] = own[c] + cgain[...] * out
            send(*corr_args(r, c))

    send_smoothed(NC)
    for c in range(COMPS):
        add = widen(corr[NC - 1, c])
        own = sweep_own([field[2, c, p] + add for p in range(2)], c)
        arrive(*corr_args(NC - 1, c))
        next_field(2, c, own, [widen(corr_halo[NC - 1, d, c]) for d in range(2)])

    drain(COMPS * PIECES)
    outs = []
    for c in range(COMPS):
        own = sweep_own([field[3, c, p] for p in range(2)], c)
        for h in range(PIECES):
            arrive(*field_args(3, c, h))
            new = sweep_rest(own, 3, c, h, None)
            for p in range(2):
                for x in range(PIECE):
                    first = c * comp_rows + 2 * (h * PIECE + x) + p
                    out_raw[pl.ds(first, NY, stride=2 * TILES), :] = new[p][x]
        done = pltpu.make_async_copy(
            out_raw.at[comp_slice(c)], out_hbm.at[comp_slice(c)], out_sem.at[c])
        done.start()
        outs.append(done)
    drain()
    for done in outs:
        done.wait()


def body(source, warm_start, coefficient):
    comps, planes, cells = source.shape
    rows = planes * cells // 128

    def flat(array):
        lead = array.shape[:-2]
        split = array.reshape(lead + (planes, cells // 128, 128))
        return jnp.swapaxes(split, -3, -2).reshape(-1, 128)

    def vm(*shape):
        return pltpu.VMEM(shape + (8, 128), jnp.float32)

    raw = pltpu.VMEM((comps * rows, 128), jnp.float32)
    out = pl.pallas_call(
        kernel,
        out_shape=jax.ShapeDtypeStruct((comps * rows, 128), jnp.float32),
        in_specs=[pl.BlockSpec(memory_space=pl.ANY)] * 3,
        out_specs=pl.BlockSpec(memory_space=pl.ANY),
        scratch_shapes=[
            raw, raw, pltpu.VMEM((rows, 128), jnp.float32), raw,
            vm(comps, 2, TILES),
            vm(4, comps, 2, TILES),
            vm(4, 2, comps, TILES),
            vm(2, TILES), vm(2, TILES),
            vm(2, TILES), vm(2, TILES), vm(TILES), vm(2, TILES), vm(2, TILES),
            vm(QUARTER), vm(2, QUARTER),
            vm(QUARTER), vm(QUARTER), vm(2, QUARTER), vm(QUARTER),
            vm(comps, 2, QUARTER), vm(comps, 2, QUARTER),
            vm(comps, QUARTER),
            vm(NC, comps, QUARTER), vm(NC, 2, comps, QUARTER),
            pltpu.SemaphoreType.DMA((1 + 2 * COMPS,)),
            pltpu.SemaphoreType.DMA((COMPS,)),
            pltpu.SemaphoreType.DMA((N_IDS, 2)),
            pltpu.SemaphoreType.DMA((N_IDS, 2)),
        ],
        compiler_params=pltpu.CompilerParams(
            collective_id=0, has_side_effects=True, vmem_limit_bytes=54528 * 1024),
    )(flat(source), flat(warm_start), flat(coefficient))
    out = out.reshape(comps, cells // 128, planes, 128)
    return jnp.swapaxes(out, 1, 2).reshape(comps, planes, cells)


def solution(mesh):
    in_specs = (P("groups", "gz", None), P("groups", "gz", None), P(("groups", "gz"), None))
    out_specs = P("groups", "gz", None)
    return jax.shard_map(body, mesh=mesh, in_specs=in_specs, out_specs=out_specs, check_vma=False)
```
